32 devices in a mesh: lat: 4 (over y, x), lon: 8 (over z, core).
Axes of the slice: x: 2, y: 2, z: 4, core: 2. Of those that a mesh axis runs over, the one named last changes fastest.
Arguments:
- tokens: bfloat16 [1, 48, 192, 512], P(None, 'lat', 'lon'), may hold values from -6 to 6
- qkv_first: bfloat16 [1536, 512], replicated, may hold values from -1 to 1, as said below
- out_first: bfloat16 [512, 512], replicated, may hold values from -0.25 to 0.25
- qkv_second: bfloat16 [1536, 512], replicated, may hold values from -1 to 1, as said below
- out_second: bfloat16 [512, 512], replicated, may hold values from -0.25 to 0.25
- merge_weight: bfloat16 [1024, 2048], replicated, may hold values from -0.125 to 0.125
- qkv_third: bfloat16 [3072, 1024], replicated, may hold values from -1 to 1, as said below
- out_third: bfloat16 [1024, 1024], replicated, may hold values from -0.1875 to 0.1875
- cotangent: bfloat16 [1, 24, 96, 1024], P(None, 'lat', 'lon'), may hold values from -6 to 6
Outputs:
- latent: bfloat16 [1, 24, 96, 1024], P(None, 'lat', 'lon')
- tokens_grad: bfloat16 [1, 48, 192, 512], P(None, 'lat', 'lon')
- qkv_first_grad: float32 [1536, 512], P(('lat', 'lon'))
- out_first_grad: float32 [512, 512], P(('lat', 'lon'))
- qkv_second_grad: float32 [1536, 512], P(('lat', 'lon'))
- out_second_grad: float32 [512, 512], P(('lat', 'lon'))
- merge_grad: float32 [1024, 2048], P(('lat', 'lon'))
- qkv_third_grad: float32 [3072, 1024], P(('lat', 'lon'))
- out_third_grad: float32 [1024, 1024], P(('lat', 'lon'))
The draws below stay inside these ranges and needn't reach their ends.
Inputs may be any that keep to these rules, and one draw needn't show every extreme that they name: `qkv_first`: a query, key and value projection, query and key rows first. `qkv_second`: a query, key and value projection, query and key rows first. `qkv_third`: a query, key and value projection, query and key rows first.
All inputs are finite; a program needn't handle non-finite values.
Results may differ from the reference program's by a relative error of at most 0.04.
Values may be sent and summed in bfloat16 or wider, within the bound.
A program may use at most 192 MiB of HBM per device.

```python
import jax
import jax.numpy as jnp
from jax import lax

C = 512
C2 = 1024
HDIM = 64
LEV = 1
WA = 6
WO = 12
LAT = 48
LON = 192
LAT2 = 24
LON2 = 96


def projection_draw(key, channels, strength_top):
    first_key, second_key, third_key = jax.random.split(key, 3)
    base = jax.random.normal(first_key, (3 * channels, channels), jnp.float32) * channels ** (-0.5)
    shared = jax.random.normal(second_key, (channels, channels), jnp.float32) * channels ** (-0.5)
    head_count = channels // HDIM
    strength = strength_top * jnp.exp(-1.8 * jax.random.uniform(third_key, (head_count,), jnp.float32))
    scaled = jnp.repeat(strength, HDIM)[:, None] * shared
    extra = jnp.concatenate([scaled, scaled, jnp.zeros((channels, channels), jnp.float32)], axis=0)
    return jnp.clip(base + extra, -1.0, 1.0).astype(jnp.bfloat16)


def draw_qkv_first(key, part):
    key = jax.random.fold_in(key, 5)
    strength_top = 0.0
    return projection_draw(key, C, strength_top)


def draw_qkv_second(key, part):
    key = jax.random.fold_in(key, 7)
    strength_top = 0.0
    return projection_draw(key, C, strength_top)


def draw_qkv_third(key, part):
    key = jax.random.fold_in(key, 9)
    strength_top = 0.0
    return projection_draw(key, C2, strength_top)


def spiked(values, key, source, target, blocks, factor):
    owner, partner = [(jnp.arange(values.shape[dim]) // (values.shape[dim] // blocks)).reshape([-1 if axis == dim else 1 for axis in range(values.ndim)]) for dim in (source, target)]
    chosen = jax.random.permutation(key, blocks)[partner]
    strong = (owner == chosen) | (owner == (partner + blocks // 2) % blocks)
    return jnp.where(strong, factor * values, values)


def shard_levels(own_key, dims, cuts, low, largest):
    def one(dim, parts):
        heights = jax.random.uniform(jax.random.fold_in(jax.random.fold_in(own_key, 6), dim), (parts,), jnp.float32, low / len(cuts), largest / len(cuts))
        return jnp.repeat(jnp.exp(heights), dims[dim] // parts).reshape((-1,) + (1,) * (len(dims) - dim - 1))

    factor_of = one(*cuts[0])
    for cut in cuts[1:]:
        factor_of = factor_of * one(*cut)
    return factor_of


def bell_draw(key, shape, spread, most, shards=(), kind=jnp.bfloat16):
    array = spread * jax.random.normal(key, shape, jnp.float32)
    if shards:
        array = array * shard_levels(key, shape, shards, -0.22, 0.18)
    return jnp.clip(array, -most, most).astype(kind)


def gaussian_with(own_key, extent, width, reach, cuts, heavy, held_as=jnp.bfloat16):
    values = width * jax.random.normal(own_key, extent, jnp.float32)
    if cuts:
        values = values * shard_levels(own_key, extent, cuts, -0.22, 0.18)
    return jnp.clip(spiked(values, jax.random.fold_in(own_key, 3), *heavy), -reach, reach).astype(held_as)


def setup_inputs(seed: int = 0) -> dict:
    streams_of = jax.random.split(jax.random.key(seed), 10)
    return {
        "tokens": bell_draw(streams_of[0], (LEV, LAT, LON, C), 1.0, 6.0, ((1, 4), (2, 8))),
        "qkv_first": draw_qkv_first(jax.random.fold_in(streams_of[9], 71), 0),
        "out_first": bell_draw(streams_of[2], (C, C), C ** -0.5, 0.25),
        "qkv_second": draw_qkv_second(jax.random.fold_in(streams_of[9], 71), 0),
        "out_second": bell_draw(streams_of[4], (C, C), C ** -0.5, 0.25),
        "merge_weight": bell_draw(streams_of[5], (C2, 4 * C), (4 * C) ** -0.5, 0.125),
        "qkv_third": draw_qkv_third(jax.random.fold_in(streams_of[9], 71), 0),
        "out_third": bell_draw(streams_of[7], (C2, C2), C2 ** -0.5, 0.1875),
        "cotangent": gaussian_with(streams_of[8], (LEV, LAT2, LON2, C2), 1.0, 6.0, ((1, 4), (2, 8)), (2, 3, 8, 2.0)),
    }


EPSILON = 1e-05

def normalize(field):
    values = field.astype(jnp.float32)
    average = lax.optimization_barrier(jnp.mean(values, axis=-1, keepdims=True))
    centered = values - average
    variance = lax.optimization_barrier(jnp.mean(centered * centered, axis=-1, keepdims=True))
    return (centered * lax.rsqrt(variance + EPSILON)).astype(jnp.bfloat16)

def project(rows, matrix):
    return lax.dot_general(rows, matrix, (((1,), (1,)), ((), ())), preferred_element_type=jnp.float32)

def grad_weight(cotan, rows):
    return lax.dot_general(cotan, rows, (((0,), (0,)), ((), ())), preferred_element_type=jnp.float32)

def pull_back(cotan, matrix):
    return jnp.dot(cotan, matrix, preferred_element_type=jnp.float32).astype(jnp.bfloat16)

def combine(first_term, second_term):
    return (first_term.astype(jnp.float32) + second_term.astype(jnp.float32)).astype(jnp.bfloat16)

def windows(field, lat_win, lon_win):
    levels, lat_rows, lon_cols, channels = field.shape
    blocked = field.reshape(levels, lat_rows // lat_win, lat_win, lon_cols // lon_win, lon_win, channels)
    blocked = blocked.transpose(1, 3, 0, 2, 4, 5)
    return blocked.reshape(lat_rows // lat_win * (lon_cols // lon_win), levels * lat_win * lon_win, channels)

def unwindows(blocks, grid_shape, lat_win, lon_win):
    levels, lat_rows, lon_cols, channels = grid_shape
    blocked = blocks.reshape(lat_rows // lat_win, lon_cols // lon_win, levels, lat_win, lon_win, channels)
    blocked = blocked.transpose(2, 0, 3, 1, 4, 5)
    return blocked.reshape(levels, lat_rows, lon_cols, channels)

def merge_patches(field):
    levels, lat_rows, lon_cols, channels = field.shape
    blocked = field.reshape(levels, lat_rows // 2, 2, lon_cols // 2, 2, channels).transpose(0, 1, 3, 4, 2, 5)
    return blocked.reshape(levels, lat_rows // 2, lon_cols // 2, 4 * channels)

def split_patches(field):
    levels, lat_half, lon_half, four_channels = field.shape
    blocked = field.reshape(levels, lat_half, lon_half, 2, 2, four_channels // 4).transpose(0, 1, 4, 2, 3, 5)
    return blocked.reshape(levels, 2 * lat_half, 2 * lon_half, four_channels // 4)

def region_bias(rows_start, lat_total, grid_shape, lat_win, lon_win):
    levels, lat_rows, lon_cols, channels = grid_shape
    row_index = rows_start + jnp.arange(lat_rows, dtype=jnp.int32)
    region = (row_index >= lat_total - lat_win).astype(jnp.float32) + (row_index >= lat_total - lat_win // 2).astype(jnp.float32)
    region_grid = jnp.broadcast_to(region[None, :, None, None], (levels, lat_rows, lon_cols, 1))
    region_tags = windows(region_grid, lat_win, lon_win)[:, :, 0]
    same = region_tags[:, :, None] == region_tags[:, None, :]
    return jnp.where(same, jnp.float32(0.0), jnp.float32(-1e+30)).astype(jnp.float32)

def attend(packed, mask_bias):
    window_count, window_size, triple_width = packed.shape
    channels = triple_width // 3
    head_count = channels // HDIM
    unpacked = packed.astype(jnp.float32).reshape(window_count, window_size, 3, head_count, HDIM)
    scores = jnp.einsum('wqhd,wkhd->whqk', unpacked[:, :, 0], unpacked[:, :, 1], precision=lax.Precision.HIGHEST)
    scores = scores * HDIM ** (-0.5) + mask_bias[:, None]
    weights = jax.nn.softmax(scores, axis=-1).astype(jnp.bfloat16)
    blended = jnp.einsum('whqk,wkhd->wqhd', weights.astype(jnp.float32), unpacked[:, :, 2], precision=lax.Precision.HIGHEST)
    return blended.reshape(window_count, window_size, channels).astype(jnp.bfloat16)

def attention_forward(field, w_qkv, w_out, mask_bias, lat_win, lon_win):
    normed, norm_back = jax.vjp(normalize, field)
    blocks = windows(normed, lat_win, lon_win)
    window_count, window_size, channels = blocks.shape
    flat_rows = blocks.reshape(window_count * window_size, channels)
    triple = project(flat_rows, w_qkv).astype(jnp.bfloat16).reshape(window_count, window_size, 3 * channels)
    blended, core_back = jax.vjp(lambda packed: attend(packed, mask_bias), triple)
    blended_flat = blended.reshape(window_count * window_size, channels)
    result = project(blended_flat, w_out).astype(jnp.bfloat16)
    result = unwindows(result.reshape(window_count, window_size, channels), field.shape, lat_win, lon_win)
    return (result, (flat_rows, blended_flat, norm_back, core_back))

def attention_backward(cotan, stored, w_qkv, w_out, grid_shape, lat_win, lon_win):
    flat_rows, blended_flat, norm_back, core_back = stored
    blocks = windows(cotan, lat_win, lon_win)
    window_count, window_size, channels = blocks.shape
    cotan_flat = blocks.reshape(window_count * window_size, channels)
    grad_out = grad_weight(cotan_flat, blended_flat)
    cotan_blended = pull_back(cotan_flat, w_out).reshape(window_count, window_size, channels)
    cotan_triple, = core_back(cotan_blended)
    triple_flat = cotan_triple.reshape(window_count * window_size, 3 * channels)
    grad_qkv = grad_weight(triple_flat, flat_rows)
    cotan_normed = pull_back(triple_flat, w_qkv).reshape(window_count, window_size, channels)
    cotan_field, = norm_back(unwindows(cotan_normed, grid_shape, lat_win, lon_win))
    return (cotan_field, (grad_qkv, grad_out))

def reference(tokens, qkv_first, out_first, qkv_second, out_second, merge_weight, qkv_third, out_third, cotangent):
    grid_shape = tokens.shape
    span = LEV * WA * WO
    no_bias = jnp.zeros((1, span, span), jnp.float32)
    first_out, first_store = attention_forward(tokens, qkv_first, out_first, no_bias, WA, WO)
    layer_one = combine(tokens, first_out)
    rolled = jnp.roll(layer_one, (-(WA // 2), -(WO // 2)), axis=(1, 2))
    mask_bias = region_bias(0, LAT, grid_shape, WA, WO)
    second_out, second_store = attention_forward(rolled, qkv_second, out_second, mask_bias, WA, WO)
    layer_two = combine(layer_one, jnp.roll(second_out, (WA // 2, WO // 2), axis=(1, 2)))
    merged = merge_patches(layer_two)
    normed, norm_back = jax.vjp(normalize, merged)
    merged_shape = normed.shape
    merged_rows = normed.reshape(-1, merged_shape[3])
    hidden = project(merged_rows, merge_weight).astype(jnp.bfloat16)
    hidden = hidden.reshape(merged_shape[0], merged_shape[1], merged_shape[2], -1)
    third_out, third_store = attention_forward(hidden, qkv_third, out_third, no_bias, WA, WO)
    latent = combine(hidden, third_out)
    third_cotan, third_grads = attention_backward(cotangent, third_store, qkv_third, out_third, hidden.shape, WA, WO)
    hidden_cotan = combine(cotangent, third_cotan)
    hidden_rows = hidden_cotan.reshape(-1, hidden.shape[3])
    merge_grad = grad_weight(hidden_rows, merged_rows)
    normed_cotan = pull_back(hidden_rows, merge_weight).reshape(merged_shape)
    merged_cotan, = norm_back(normed_cotan)
    two_cotan = split_patches(merged_cotan)
    second_cotan = jnp.roll(two_cotan, (-(WA // 2), -(WO // 2)), axis=(1, 2))
    rolled_cotan, second_grads = attention_backward(second_cotan, second_store, qkv_second, out_second, grid_shape, WA, WO)
    one_cotan = combine(two_cotan, jnp.roll(rolled_cotan, (WA // 2, WO // 2), axis=(1, 2)))
    first_cotan, first_grads = attention_backward(one_cotan, first_store, qkv_first, out_first, grid_shape, WA, WO)
    tokens_grad = combine(one_cotan, first_cotan)
    return (latent, tokens_grad, first_grads[0], first_grads[1], second_grads[0], second_grads[1], merge_grad, third_grads[0], third_grads[1])
```

```python
import jax
import jax.numpy as jnp
from jax import lax
from jax.sharding import PartitionSpec as P

HDIM = 64
LEV = 1
WA = 6
WO = 12


EPSILON = 1e-05


def from_behind(block, axis, distance):
    devices = range(lax.axis_size(axis))
    route = [((i - distance) % len(devices), i) for i in devices]
    return lax.ppermute(block, axis, route)


def normalize(field):
    values = field.astype(jnp.float32)
    average = jnp.mean(values, axis=-1, keepdims=True)
    centered = values - average
    variance = jnp.mean(centered * centered, axis=-1, keepdims=True)
    return (centered * lax.rsqrt(variance + EPSILON)).astype(jnp.bfloat16)


def project(rows, matrix):
    return lax.dot_general(
        rows, matrix, (((1,), (1,)), ((), ())), preferred_element_type=jnp.float32
    )


def grad_weight(cotan, rows):
    return lax.dot_general(
        cotan, rows, (((0,), (0,)), ((), ())), preferred_element_type=jnp.float32
    )


def pull_back(cotan, matrix):
    return jnp.dot(cotan, matrix, preferred_element_type=jnp.float32).astype(jnp.bfloat16)


def combine(first_term, second_term):
    return (first_term.astype(jnp.float32) + second_term.astype(jnp.float32)).astype(jnp.bfloat16)


def windows(field, lat_win, lon_win):
    levels, lat_rows, lon_cols, channels = field.shape
    blocked = field.reshape(
        levels, lat_rows // lat_win, lat_win, lon_cols // lon_win, lon_win, channels
    )
    blocked = blocked.transpose(1, 3, 0, 2, 4, 5)
    return blocked.reshape(
        lat_rows // lat_win * (lon_cols // lon_win), levels * lat_win * lon_win, channels
    )


def unwindows(blocks, grid_shape, lat_win, lon_win):
    levels, lat_rows, lon_cols, channels = grid_shape
    blocked = blocks.reshape(
        lat_rows // lat_win, lon_cols // lon_win, levels, lat_win, lon_win, channels
    )
    blocked = blocked.transpose(2, 0, 3, 1, 4, 5)
    return blocked.reshape(levels, lat_rows, lon_cols, channels)


def merge_patches(field):
    levels, lat_rows, lon_cols, channels = field.shape
    blocked = field.reshape(levels, lat_rows // 2, 2, lon_cols // 2, 2, channels).transpose(
        0, 1, 3, 4, 2, 5
    )
    return blocked.reshape(levels, lat_rows // 2, lon_cols // 2, 4 * channels)


def split_patches(field):
    levels, lat_half, lon_half, four_channels = field.shape
    blocked = field.reshape(levels, lat_half, lon_half, 2, 2, four_channels // 4).transpose(
        0, 1, 4, 2, 3, 5
    )
    return blocked.reshape(levels, 2 * lat_half, 2 * lon_half, four_channels // 4)


def region_bias(rows_start, lat_total, grid_shape, lat_win, lon_win):
    levels, lat_rows, lon_cols, channels = grid_shape
    row_index = rows_start + jnp.arange(lat_rows, dtype=jnp.int32)
    region = (row_index >= lat_total - lat_win).astype(jnp.float32) + (
        row_index >= lat_total - lat_win // 2
    ).astype(jnp.float32)
    region_grid = jnp.broadcast_to(region[None, :, None, None], (levels, lat_rows, lon_cols, 1))
    region_tags = windows(region_grid, lat_win, lon_win)[:, :, 0]
    same = region_tags[:, :, None] == region_tags[:, None, :]
    return jnp.where(same, jnp.float32(0.0), jnp.float32(-1e30))


def split_product(form, wide, narrow):
    upper = wide.astype(jnp.bfloat16)
    lower = (wide - upper.astype(jnp.float32)).astype(jnp.bfloat16)
    first_part = jnp.einsum(form, upper, narrow, preferred_element_type=jnp.float32)
    return first_part + jnp.einsum(form, lower, narrow, preferred_element_type=jnp.float32)


def attend_forward(packed, mask_bias):
    window_count, window_size, triple_width = packed.shape
    channels = triple_width // 3
    head_count = channels // HDIM
    scale = HDIM ** (-0.5)
    unpacked = packed.reshape(window_count, window_size, 3, head_count, HDIM)
    queries = unpacked[:, :, 0]
    keys_all = unpacked[:, :, 1]
    values_all = unpacked[:, :, 2]
    scores = jnp.einsum("wqhd,wkhd->whqk", queries, keys_all, preferred_element_type=jnp.float32)
    scores = scores * scale + mask_bias[:, None]
    probs = jax.nn.softmax(scores, axis=-1)
    weights = probs.astype(jnp.bfloat16)
    blended = jnp.einsum("whqk,wkhd->wqhd", weights, values_all, preferred_element_type=jnp.float32)
    blended = blended.reshape(window_count, window_size, channels).astype(jnp.bfloat16)

    def core_back(cotan):
        cotan_heads = cotan.reshape(window_count, window_size, head_count, HDIM)
        cotan_weights = jnp.einsum(
            "wqhd,wkhd->whqk", cotan_heads, values_all, preferred_element_type=jnp.float32
        )
        cotan_weights = cotan_weights.astype(jnp.bfloat16).astype(jnp.float32)
        inner = jnp.sum(probs * cotan_weights, axis=-1, keepdims=True)
        cotan_scores = probs * (cotan_weights - inner) * scale
        cotan_queries = split_product("whqk,wkhd->wqhd", cotan_scores, keys_all)
        cotan_keys = split_product("whqk,wqhd->wkhd", cotan_scores, queries)
        cotan_values = jnp.einsum(
            "whqk,wqhd->wkhd", weights, cotan_heads, preferred_element_type=jnp.float32
        )
        stacked = jnp.stack(
            [
                cotan_queries.astype(jnp.bfloat16),
                cotan_keys.astype(jnp.bfloat16),
                cotan_values.astype(jnp.bfloat16),
            ],
            axis=2,
        )
        return (stacked.reshape(window_count, window_size, triple_width),)

    return (blended, core_back)


def attention_forward(field, w_qkv, w_out, mask_bias, lat_win, lon_win):
    normed, norm_back = jax.vjp(normalize, field)
    blocks = windows(normed, lat_win, lon_win)
    window_count, window_size, channels = blocks.shape
    flat_rows = blocks.reshape(window_count * window_size, channels)
    triple = (
        project(flat_rows, w_qkv)
        .astype(jnp.bfloat16)
        .reshape(window_count, window_size, 3 * channels)
    )
    blended, core_back = attend_forward(triple, mask_bias)
    blended_flat = blended.reshape(window_count * window_size, channels)
    result = project(blended_flat, w_out).astype(jnp.bfloat16)
    result = unwindows(
        result.reshape(window_count, window_size, channels), field.shape, lat_win, lon_win
    )
    return (result, (flat_rows, blended_flat, norm_back, core_back))


def attention_backward(cotan, stored, w_qkv, w_out, grid_shape, lat_win, lon_win):
    flat_rows, blended_flat, norm_back, core_back = stored
    blocks = windows(cotan, lat_win, lon_win)
    window_count, window_size, channels = blocks.shape
    cotan_flat = blocks.reshape(window_count * window_size, channels)
    grad_out = grad_weight(cotan_flat, blended_flat)
    cotan_blended = pull_back(cotan_flat, w_out).reshape(window_count, window_size, channels)
    (cotan_triple,) = core_back(cotan_blended)
    triple_flat = cotan_triple.reshape(window_count * window_size, 3 * channels)
    grad_qkv = grad_weight(triple_flat, flat_rows)
    cotan_normed = pull_back(triple_flat, w_qkv).reshape(window_count, window_size, channels)
    (cotan_field,) = norm_back(unwindows(cotan_normed, grid_shape, lat_win, lon_win))
    return (cotan_field, (grad_qkv, grad_out))


def roll_ahead(field):
    half_lat = WA // 2
    half_lon = WO // 2
    incoming = from_behind(field[:, :half_lat], "lat", -1)
    field = jnp.concatenate([field[:, half_lat:], incoming], axis=1)
    incoming = from_behind(field[:, :, :half_lon], "lon", -1)
    return jnp.concatenate([field[:, :, half_lon:], incoming], axis=2)


def roll_behind(field):
    half_lat = WA // 2
    half_lon = WO // 2
    incoming = from_behind(field[:, -half_lat:], "lat", 1)
    field = jnp.concatenate([incoming, field[:, :-half_lat]], axis=1)
    incoming = from_behind(field[:, :, -half_lon:], "lon", 1)
    return jnp.concatenate([incoming, field[:, :, :-half_lon]], axis=2)


def exchanged(pieces, axis, mine, partner_of, dim):
    keep = lax.dynamic_index_in_dim(pieces, mine, dim, keepdims=False)
    send = lax.dynamic_index_in_dim(pieces, 1 - mine, dim, keepdims=False)
    route = [(i, partner_of(i)) for i in range(lax.axis_size(axis))]
    return combine(keep, lax.ppermute(send, axis, route))


def scatter_sum(grad, low_first):
    lat_size, lon_size = lax.axis_size("lat"), lax.axis_size("lon")
    lat, lon = lax.axis_index("lat"), lax.axis_index("lon")
    bits = lat_size.bit_length() - 1
    chips = lon_size // 2
    pieces = grad.reshape((2,) * bits + (chips, 2) + grad.shape[1:])
    pieces = exchanged(pieces, "lon", lon % 2, lambda i: i ^ 1, bits + 1)
    left = list(range(bits))
    for bit in range(bits) if low_first else reversed(range(bits)):
        dim = left.index(bits - 1 - bit)
        left.pop(dim)
        mine = lax.div(lat, jnp.int32(2**bit)) % 2
        pieces = exchanged(pieces, "lat", mine, lambda i: i ^ 2**bit, dim)
    chip = lon // 2
    total = lax.dynamic_index_in_dim(pieces, chip, 0, keepdims=False).astype(jnp.float32)
    for step in range(1, chips):
        send = lax.dynamic_index_in_dim(pieces, (chip + step) % chips, 0, keepdims=False)
        route = [(i, (i + 2 * step) % lon_size) for i in range(lon_size)]
        total = total + lax.ppermute(send, "lon", route).astype(jnp.float32)
    return total


def blocks_of(grad):
    devices = lax.axis_size("lat") * lax.axis_size("lon")
    return grad.astype(jnp.bfloat16).reshape(devices, grad.shape[0] // devices, grad.shape[1])


def scatter_pair(grad_qkv, grad_out, low_first):
    total = scatter_sum(
        jnp.concatenate([blocks_of(grad_qkv), blocks_of(grad_out)], axis=1), low_first
    )
    cut = total.shape[0] * 3 // 4
    return total[:cut], total[cut:]


def scatter_merge(merge_grad, grad_out):
    blocks = blocks_of(merge_grad)
    half = blocks.shape[2] // 2
    stacked = jnp.concatenate(
        [blocks[:, :, :half], blocks[:, :, half:], blocks_of(grad_out)], axis=1
    )
    first, second, out = jnp.split(scatter_sum(stacked, False), 3, axis=0)
    return jnp.concatenate([first, second], axis=1), out


def on_device(
    tokens,
    qkv_first,
    out_first,
    qkv_second,
    out_second,
    merge_weight,
    qkv_third,
    out_third,
    cotangent,
):
    grid_shape = tokens.shape
    span = LEV * WA * WO
    no_bias = jnp.zeros((1, span, span), jnp.float32)
    first_out, first_store = attention_forward(tokens, qkv_first, out_first, no_bias, WA, WO)
    layer_one = combine(tokens, first_out)
    rolled = roll_ahead(layer_one)
    tile_rows = grid_shape[1]
    mask_bias = region_bias(
        lax.axis_index("lat") * tile_rows, tile_rows * lax.axis_size("lat"), grid_shape, WA, WO
    )
    second_out, second_store = attention_forward(rolled, qkv_second, out_second, mask_bias, WA, WO)
    layer_two = combine(layer_one, roll_behind(second_out))
    merged = merge_patches(layer_two)
    normed, norm_back = jax.vjp(normalize, merged)
    merged_shape = normed.shape
    merged_rows = normed.reshape(-1, merged_shape[3])
    hidden = project(merged_rows, merge_weight).astype(jnp.bfloat16)
    hidden = hidden.reshape(merged_shape[0], merged_shape[1], merged_shape[2], -1)
    third_out, third_store = attention_forward(hidden, qkv_third, out_third, no_bias, WA, WO)
    latent = combine(hidden, third_out)
    third_cotan, third_grads = attention_backward(
        cotangent, third_store, qkv_third, out_third, hidden.shape, WA, WO
    )
    hidden_cotan = combine(cotangent, third_cotan)
    hidden_rows = hidden_cotan.reshape(-1, hidden.shape[3])
    merge_grad = grad_weight(hidden_rows, merged_rows)
    normed_cotan = pull_back(hidden_rows, merge_weight).reshape(merged_shape)
    (merged_cotan,) = norm_back(normed_cotan)
    two_cotan = split_patches(merged_cotan)
    second_cotan = roll_ahead(two_cotan)
    rolled_cotan, second_grads = attention_backward(
        second_cotan, second_store, qkv_second, out_second, grid_shape, WA, WO
    )
    one_cotan = combine(two_cotan, roll_behind(rolled_cotan))
    first_cotan, first_grads = attention_backward(
        one_cotan, first_store, qkv_first, out_first, grid_shape, WA, WO
    )
    tokens_grad = combine(one_cotan, first_cotan)
    third_share = scatter_sum(blocks_of(third_grads[0]), True)
    merge_share, third_out_share = scatter_merge(merge_grad, third_grads[1])
    second_shares = scatter_pair(*second_grads, True)
    first_shares = scatter_pair(*first_grads, False)
    shares = (*first_shares, *second_shares, merge_share, third_share, third_out_share)
    return (
        latent,
        tokens_grad,
        shares[0],
        shares[1],
        shares[2],
        shares[3],
        shares[4],
        shares[5],
        shares[6],
    )


def solution(mesh):
    placed = (
        P(None, "lat", "lon", None),
        P(),
        P(),
        P(),
        P(),
        P(),
        P(),
        P(),
        P(None, "lat", "lon", None),
    )
    return jax.shard_map(
        on_device,
        mesh=mesh,
        in_specs=placed,
        out_specs=(
            P(None, "lat", "lon", None),
            P(None, "lat", "lon", None),
            P(("lat", "lon"), None),
            P(("lat", "lon"), None),
            P(("lat", "lon"), None),
            P(("lat", "lon"), None),
            P(("lat", "lon"), None),
            P(("lat", "lon"), None),
            P(("lat", "lon"), None),
        ),
        check_vma=False,
    )
```

```python
import functools

import jax
import jax.numpy as jnp
from jax import lax
from jax.experimental import pallas as pl
from jax.experimental.pallas import tpu as pltpu
from jax.sharding import PartitionSpec as P

HDIM = 64
LEV = 1
WA = 6
WO = 12
SPAN = LEV * WA * WO
SLOT = 80
HEADS = 4
WIDE = HEADS * HDIM
BLOCKED = -1e30

EPSILON = 1e-05


def combine(first_term, second_term):
    return (first_term.astype(jnp.float32) + second_term.astype(jnp.float32)).astype(jnp.bfloat16)


def windows(field):
    lat_rows, lon_cols, channels = field.shape
    blocked = field.reshape(lat_rows // WA, WA, lon_cols // WO, WO, channels)
    blocked = blocked.transpose(0, 2, 1, 3, 4).reshape(-1, SPAN, channels)
    return jnp.pad(blocked, ((0, 0), (0, SLOT - SPAN), (0, 0))).reshape(-1, channels)


def unwindows(blocks, lat_rows, lon_cols):
    channels = blocks.shape[-1]
    blocked = blocks.reshape(-1, SLOT, channels)[:, :SPAN]
    blocked = blocked.reshape(lat_rows // WA, lon_cols // WO, WA, WO, channels)
    return blocked.transpose(0, 2, 1, 3, 4).reshape(lat_rows, lon_cols, channels)


def merge_patches(field):
    lat_rows, lon_cols, channels = field.shape
    blocked = field.reshape(lat_rows // 2, 2, lon_cols // 2, 2, channels).transpose(0, 2, 3, 1, 4)
    return blocked.reshape(lat_rows // 2, lon_cols // 2, 4 * channels)


def split_patches(field):
    lat_half, lon_half, four_channels = field.shape
    blocked = field.reshape(lat_half, lon_half, 2, 2, four_channels // 4).transpose(0, 3, 1, 2, 4)
    return blocked.reshape(2 * lat_half, 2 * lon_half, four_channels // 4)


def from_behind(block, axis, distance):
    size = lax.axis_size(axis)
    return lax.ppermute(block, axis, [((i - distance) % size, i) for i in range(size)])


def from_corner(block, distance):
    lats, lons = lax.axis_size("lat"), lax.axis_size("lon")
    route = [
        ((i - distance) % lats * lons + (j - distance) % lons, i * lons + j)
        for i in range(lats)
        for j in range(lons)
    ]
    return lax.ppermute(block, ("lat", "lon"), route)


def roll_ahead(field):
    low, west = WA // 2, WO // 2
    corner = from_corner(field[:low, :west], -1)
    below = from_behind(field[:low, west:], "lat", -1)
    beside = from_behind(field[low:, :west], "lon", -1)
    upper = jnp.concatenate([field[low:, west:], beside], axis=1)
    return jnp.concatenate([upper, jnp.concatenate([below, corner], axis=1)], axis=0)


def roll_behind(field):
    low, west = WA // 2, WO // 2
    corner = from_corner(field[-low:, -west:], 1)
    above = from_behind(field[-low:, :-west], "lat", 1)
    beside = from_behind(field[:-low, -west:], "lon", 1)
    lower = jnp.concatenate([beside, field[:-low, :-west]], axis=1)
    return jnp.concatenate([jnp.concatenate([corner, above], axis=1), lower], axis=0)


def dot(left, right, left_dim=1, right_dim=0):
    return lax.dot_general(
        left, right, (((left_dim,), (right_dim,)), ((), ())), preferred_element_type=jnp.float32
    )


def centre(field):
    values = field.astype(jnp.float32)
    centered = values - jnp.mean(values, axis=-1, keepdims=True)
    inverse = lax.rsqrt(jnp.mean(centered * centered, axis=-1, keepdims=True) + EPSILON)
    return centered * inverse, inverse


def norm_back(field, cotan):
    scaled, inverse = centre(field)
    cotan = cotan.astype(jnp.float32)
    along = jnp.mean(cotan * scaled, axis=-1, keepdims=True)
    return (inverse * (cotan - jnp.mean(cotan, axis=-1, keepdims=True) - scaled * along)).astype(
        jnp.bfloat16
    )


def head_mask(head):
    lane = lax.broadcasted_iota(jnp.int32, (1, WIDE), 1)
    return jnp.where((lane >= head * HDIM) & (lane < (head + 1) * HDIM), 1.0, 0.0)


def by_head(block):
    return jnp.concatenate(
        [block * head_mask(head).astype(jnp.bfloat16) for head in range(HEADS)], axis=0
    )


def together(stacked):
    parts = [stacked[h * SLOT : (h + 1) * SLOT] * head_mask(h) for h in range(HEADS)]
    return functools.reduce(jnp.add, parts).astype(jnp.bfloat16)


def window_bias(last):
    row = lax.broadcasted_iota(jnp.int32, (SLOT, SLOT), 0)
    col = lax.broadcasted_iota(jnp.int32, (SLOT, SLOT), 1)
    bias = jnp.zeros((SLOT, SLOT), jnp.float32)
    if last is not None:
        half = LEV * (WA // 2) * WO
        same = ((row < half) & (col < half)) | ((row >= half) & (col >= half))
        bias = jnp.where(same, 0.0, BLOCKED * last)
    bias = jnp.where(col < SPAN, bias, BLOCKED)
    return jnp.concatenate([bias] * HEADS, axis=0)


def softmax(queries, keys_all, bias):
    scores = dot(queries, keys_all, 1, 1) * HDIM ** (-0.5) + bias
    raised = jnp.exp(scores - jnp.max(scores, axis=-1, keepdims=True))
    return raised / jnp.sum(raised, axis=-1, keepdims=True)


def project_into(target, rows, matrix):
    step = min(512, matrix.shape[0])
    for start in range(0, matrix.shape[0], step):
        part = dot(rows, matrix[start : start + step, :], 1, 1)
        target[:, start : start + step] = part.astype(jnp.bfloat16)


def grad_into(target, cotan, rows):
    step = min(256, target.shape[0])
    for start in range(0, target.shape[0], step):
        part = dot(cotan[:, start : start + step], rows, 0, 0)
        target[start : start + step, :] = part.astype(jnp.bfloat16)


def groups(row_count, channels, lat_windows, last):
    count = row_count // SLOT
    plain = window_bias(None)
    for window in range(count):
        edge = last is not None and window // (count // lat_windows) == lat_windows - 1
        bias = window_bias(last) if edge else plain
        rows = slice(window * SLOT, (window + 1) * SLOT)
        for start in range(0, channels, WIDE):
            yield rows, start, bias


def forward_kernel(lat_windows, shifted, last_ref, x_ref, qkv_ref, out_ref, y_ref, triple, blended):
    last = last_ref[0] if shifted else None
    row_count, channels = x_ref.shape
    project_into(triple, centre(x_ref[...])[0].astype(jnp.bfloat16), qkv_ref)
    for rows, start, bias in groups(row_count, channels, lat_windows, last):
        queries, keys_all, values_all = [
            triple[rows, part * channels + start : part * channels + start + WIDE]
            for part in range(3)
        ]
        weights = softmax(by_head(queries), keys_all, bias).astype(jnp.bfloat16)
        blended[rows, start : start + WIDE] = together(dot(weights, values_all))
    result = dot(blended[...], out_ref[...], 1, 1).astype(jnp.bfloat16)
    y_ref[...] = combine(x_ref[...], result)


def block_back(
    lat_windows, last, x, cotan, qkv_ref, out_ref, qkv_grad, out_grad, triple, blended, back
):
    row_count, channels = x.shape
    rows_in = centre(x)[0].astype(jnp.bfloat16)
    project_into(triple, rows_in, qkv_ref)
    cotan_blended = dot(cotan, out_ref[...]).astype(jnp.bfloat16)
    for rows, start, bias in groups(row_count, channels, lat_windows, last):
        spots = [slice(p * channels + start, p * channels + start + WIDE) for p in range(3)]
        queries = by_head(triple[rows, spots[0]])
        keys_all, values_all = triple[rows, spots[1]], triple[rows, spots[2]]
        probs = softmax(queries, keys_all, bias)
        weights = probs.astype(jnp.bfloat16)
        blended[rows, start : start + WIDE] = together(dot(weights, values_all))
        cotan_heads = by_head(cotan_blended[rows, start : start + WIDE])
        cotan_weights = dot(cotan_heads, values_all, 1, 1)
        inner = jnp.sum(probs * cotan_weights, axis=-1, keepdims=True)
        cotan_scores = (probs * (cotan_weights - inner) * HDIM ** (-0.5)).astype(jnp.bfloat16)
        back[rows, spots[0]] = together(dot(cotan_scores, keys_all))
        back[rows, spots[1]] = dot(cotan_scores, queries, 0, 0).astype(jnp.bfloat16)
        back[rows, spots[2]] = dot(weights, cotan_heads, 0, 0).astype(jnp.bfloat16)
    grad_into(qkv_grad, back, rows_in)
    grad_into(out_grad, cotan, blended[...])
    cotan_rows = dot(back[...], qkv_ref[...]).astype(jnp.bfloat16)
    return combine(cotan, norm_back(x, cotan_rows))


def backward_kernel(
    lat_windows, shifted, last_ref, x_ref, cotan_ref, qkv_ref, out_ref,
    cotan_x_ref, qkv_grad, out_grad, triple, blended, back,
):
    last = last_ref[0] if shifted else None
    cotan_x_ref[...] = block_back(
        lat_windows, last, x_ref[...], cotan_ref[...], qkv_ref, out_ref,
        qkv_grad, out_grad, triple, blended, back,
    )


def middle_kernel(
    lat_windows, merged_ref, cotan_ref, merge_ref, qkv_ref, out_ref,
    latent_ref, cotan_merged_ref, merge_grad, qkv_grad, out_grad,
    hidden, triple, blended, back,
):
    merged_rows = centre(merged_ref[...])[0].astype(jnp.bfloat16)
    project_into(hidden, merged_rows, merge_ref)
    cotan_hidden = block_back(
        lat_windows, None, hidden[...], cotan_ref[...], qkv_ref, out_ref,
        qkv_grad, out_grad, triple, blended, back,
    )
    result = dot(blended[...], out_ref[...], 1, 1).astype(jnp.bfloat16)
    latent_ref[...] = combine(hidden[...], result)
    grad_into(merge_grad, cotan_hidden, merged_rows)
    cotan_rows = dot(cotan_hidden, merge_ref[...]).astype(jnp.bfloat16)
    cotan_merged_ref[...] = norm_back(merged_ref[...], cotan_rows)


def call(kernel, arrays, outs, scratch, flops, name, scalar_first=True):
    specs = [pl.BlockSpec(memory_space=pltpu.VMEM)] * len(arrays)
    if scalar_first:
        specs[0] = pl.BlockSpec(memory_space=pltpu.SMEM)
    shapes = [jax.ShapeDtypeStruct(shape, jnp.bfloat16) for shape in outs]
    moved = sum(a.size * a.dtype.itemsize for a in arrays) + sum(2 * s[0] * s[1] for s in outs)
    return pl.pallas_call(
        kernel,
        out_shape=shapes,
        in_specs=specs,
        out_specs=[pl.BlockSpec(memory_space=pltpu.VMEM)] * len(outs),
        scratch_shapes=[pltpu.VMEM(shape, jnp.bfloat16) for shape in scratch],
        compiler_params=pltpu.CompilerParams(vmem_limit_bytes=52 * 2**20),
        cost_estimate=pl.CostEstimate(flops=flops, bytes_accessed=moved, transcendentals=0),
        name=name,
    )(*arrays)


def block_forward(last, rows, w_qkv, w_out, lat_windows, shifted):
    count, channels = rows.shape
    return call(
        functools.partial(forward_kernel, lat_windows, shifted),
        [last, rows, w_qkv, w_out],
        [rows.shape],
        [(count, 3 * channels), rows.shape],
        8 * count * channels * channels,
        "block_forward",
    )[0]


def block_backward(last, rows, cotan, w_qkv, w_out, lat_windows, shifted):
    count, channels = rows.shape
    return call(
        functools.partial(backward_kernel, lat_windows, shifted),
        [last, rows, cotan, w_qkv, w_out],
        [rows.shape, w_qkv.shape, w_out.shape],
        [(count, 3 * channels), rows.shape, (count, 3 * channels)],
        24 * count * channels * channels,
        "block_backward",
    )


def middle(merged, cotan, w_merge, w_qkv, w_out, lat_windows):
    count, channels = cotan.shape
    return call(
        functools.partial(middle_kernel, lat_windows),
        [merged, cotan, w_merge, w_qkv, w_out],
        [cotan.shape, merged.shape, w_merge.shape, w_qkv.shape, w_out.shape],
        [cotan.shape, (count, 3 * channels), cotan.shape, (count, 3 * channels)],
        36 * count * channels * channels,
        "middle",
        False,
    )


def exchanged(pieces, axis, mine, partner_of, dim):
    keep = lax.dynamic_index_in_dim(pieces, mine, dim, keepdims=False)
    send = lax.dynamic_index_in_dim(pieces, 1 - mine, dim, keepdims=False)
    route = [(i, partner_of(i)) for i in range(lax.axis_size(axis))]
    return combine(keep, lax.ppermute(send, axis, route))


def scatter_sum(grad, low_first):
    lat_size, lon_size = lax.axis_size("lat"), lax.axis_size("lon")
    lat, lon = lax.axis_index("lat"), lax.axis_index("lon")
    bits = lat_size.bit_length() - 1
    chips = lon_size // 2
    pieces = grad.reshape((2,) * bits + (chips, 2) + grad.shape[1:])
    pieces = exchanged(pieces, "lon", lon % 2, lambda i: i ^ 1, bits + 1)
    left = list(range(bits))
    for bit in range(bits) if low_first else reversed(range(bits)):
        dim = left.index(bits - 1 - bit)
        left.pop(dim)
        mine = lax.div(lat, jnp.int32(2**bit)) % 2
        pieces = exchanged(pieces, "lat", mine, lambda i: i ^ 2**bit, dim)
    chip = lon // 2
    total = lax.dynamic_index_in_dim(pieces, chip, 0, keepdims=False).astype(jnp.float32)
    for step in range(1, chips):
        send = lax.dynamic_index_in_dim(pieces, (chip + step) % chips, 0, keepdims=False)
        route = [(i, (i + 2 * step) % lon_size) for i in range(lon_size)]
        total = total + lax.ppermute(send, "lon", route).astype(jnp.float32)
    return total


def blocks_of(grad):
    devices = lax.axis_size("lat") * lax.axis_size("lon")
    return grad.astype(jnp.bfloat16).reshape(devices, grad.shape[0] // devices, grad.shape[1])


def scatter_pair(grad_qkv, grad_out, low_first):
    total = scatter_sum(
        jnp.concatenate([blocks_of(grad_qkv), blocks_of(grad_out)], axis=1), low_first
    )
    cut = total.shape[0] * 3 // 4
    return total[:cut], total[cut:]


def scatter_merge(merge_grad, grad_out):
    blocks = blocks_of(merge_grad)
    half = blocks.shape[2] // 2
    stacked = jnp.concatenate(
        [blocks[:, :, :half], blocks[:, :, half:], blocks_of(grad_out)], axis=1
    )
    first, second, out = jnp.split(scatter_sum(stacked, False), 3, axis=0)
    return jnp.concatenate([first, second], axis=1), out


def on_device(
    tokens,
    qkv_first,
    out_first,
    qkv_second,
    out_second,
    merge_weight,
    qkv_third,
    out_third,
    cotangent,
):
    lat_rows, lon_cols = tokens.shape[1:3]
    tall = lat_rows // WA
    last = (lax.axis_index("lat") == lax.axis_size("lat") - 1).astype(jnp.float32).reshape(1)

    rows_one = windows(tokens[0])
    layer_one = block_forward(last, rows_one, qkv_first, out_first, tall, False)
    rows_two = windows(roll_ahead(unwindows(layer_one, lat_rows, lon_cols)))
    layer_two = block_forward(last, rows_two, qkv_second, out_second, tall, True)
    layer_two = roll_behind(unwindows(layer_two, lat_rows, lon_cols))
    merged = windows(merge_patches(layer_two))
    latent, merged_cotan, merge_grad, third_qkv_grad, third_out_grad = middle(
        merged, windows(cotangent[0]), merge_weight, qkv_third, out_third, tall // 2
    )
    latent = unwindows(latent, lat_rows // 2, lon_cols // 2)[None]
    third_share = scatter_sum(blocks_of(third_qkv_grad), True)
    merge_share, third_out_share = scatter_merge(merge_grad, third_out_grad)

    two_cotan = split_patches(unwindows(merged_cotan, lat_rows // 2, lon_cols // 2))
    two_cotan, *second_grads = block_backward(
        last, rows_two, windows(roll_ahead(two_cotan)), qkv_second, out_second, tall, True
    )
    second_shares = scatter_pair(*second_grads, True)
    one_cotan = windows(roll_behind(unwindows(two_cotan, lat_rows, lon_cols)))
    one_cotan, *first_grads = block_backward(
        last, rows_one, one_cotan, qkv_first, out_first, tall, False
    )
    tokens_grad = unwindows(one_cotan, lat_rows, lon_cols)[None]
    first_shares = scatter_pair(*first_grads, False)
    shares = (*first_shares, *second_shares, merge_share, third_share, third_out_share)
    return (latent, tokens_grad, *shares)


def solution(mesh):
    placed = (
        P(None, "lat", "lon", None),
        P(),
        P(),
        P(),
        P(),
        P(),
        P(),
        P(),
        P(None, "lat", "lon", None),
    )
    return jax.shard_map(
        on_device,
        mesh=mesh,
        in_specs=placed,
        out_specs=(
            P(None, "lat", "lon", None),
            P(None, "lat", "lon", None),
            P(("lat", "lon"), None),
            P(("lat", "lon"), None),
            P(("lat", "lon"), None),
            P(("lat", "lon"), None),
            P(("lat", "lon"), None),
            P(("lat", "lon"), None),
            P(("lat", "lon"), None),
        ),
        check_vma=False,
    )
```

```python
import functools
import math

import jax
import jax.numpy as jnp
from jax import lax
from jax.experimental import pallas as pl
from jax.experimental.pallas import tpu as pltpu
from jax.sharding import PartitionSpec as P

HDIM = 64
LEV = 1
WA = 6
WO = 12
SPAN = LEV * WA * WO
SLOT = 80
HEADS = 4
WIDE = HEADS * HDIM
BLOCKED = -1e30

EPSILON = 1e-05


def combine(first_term, second_term):
    return (first_term.astype(jnp.float32) + second_term.astype(jnp.float32)).astype(jnp.bfloat16)


def windows(field):
    lat_rows, lon_cols, channels = field.shape
    blocked = field.reshape(lat_rows // WA, WA, lon_cols // WO, WO, channels)
    blocked = blocked.transpose(0, 2, 1, 3, 4).reshape(-1, SPAN, channels)
    return jnp.pad(blocked, ((0, 0), (0, SLOT - SPAN), (0, 0))).reshape(-1, channels)


def unwindows(blocks, lat_rows, lon_cols):
    channels = blocks.shape[-1]
    blocked = blocks.reshape(-1, SLOT, channels)[:, :SPAN]
    blocked = blocked.reshape(lat_rows // WA, lon_cols // WO, WA, WO, channels)
    return blocked.transpose(0, 2, 1, 3, 4).reshape(lat_rows, lon_cols, channels)


def merge_patches(field):
    lat_rows, lon_cols, channels = field.shape
    blocked = field.reshape(lat_rows // 2, 2, lon_cols // 2, 2, channels).transpose(0, 2, 3, 1, 4)
    return blocked.reshape(lat_rows // 2, lon_cols // 2, 4 * channels)


def split_patches(field):
    lat_half, lon_half, four_channels = field.shape
    blocked = field.reshape(lat_half, lon_half, 2, 2, four_channels // 4).transpose(0, 3, 1, 2, 4)
    return blocked.reshape(2 * lat_half, 2 * lon_half, four_channels // 4)


def from_behind(block, axis, distance):
    size = lax.axis_size(axis)
    return lax.ppermute(block, axis, [((i - distance) % size, i) for i in range(size)])


def from_corner(block, distance):
    lats, lons = lax.axis_size("lat"), lax.axis_size("lon")
    route = [
        ((i - distance) % lats * lons + (j - distance) % lons, i * lons + j)
        for i in range(lats)
        for j in range(lons)
    ]
    return lax.ppermute(block, ("lat", "lon"), route)


def roll_ahead(field):
    low, west = WA // 2, WO // 2
    corner = from_corner(field[:low, :west], -1)
    below = from_behind(field[:low, west:], "lat", -1)
    beside = from_behind(field[low:, :west], "lon", -1)
    upper = jnp.concatenate([field[low:, west:], beside], axis=1)
    return jnp.concatenate([upper, jnp.concatenate([below, corner], axis=1)], axis=0)


def roll_behind(field):
    low, west = WA // 2, WO // 2
    corner = from_corner(field[-low:, -west:], 1)
    above = from_behind(field[-low:, :-west], "lat", 1)
    beside = from_behind(field[:-low, -west:], "lon", 1)
    lower = jnp.concatenate([beside, field[:-low, :-west]], axis=1)
    return jnp.concatenate([jnp.concatenate([corner, above], axis=1), lower], axis=0)


def dot(left, right, left_dim=1, right_dim=0):
    return lax.dot_general(
        left, right, (((left_dim,), (right_dim,)), ((), ())), preferred_element_type=jnp.float32
    )


def centre(field):
    values = field.astype(jnp.float32)
    centered = values - jnp.mean(values, axis=-1, keepdims=True)
    inverse = lax.rsqrt(jnp.mean(centered * centered, axis=-1, keepdims=True) + EPSILON)
    return centered * inverse, inverse


def norm_back(field, cotan):
    scaled, inverse = centre(field)
    cotan = cotan.astype(jnp.float32)
    along = jnp.mean(cotan * scaled, axis=-1, keepdims=True)
    return (inverse * (cotan - jnp.mean(cotan, axis=-1, keepdims=True) - scaled * along)).astype(
        jnp.bfloat16
    )


def head_mask(head):
    lane = lax.broadcasted_iota(jnp.int32, (1, WIDE), 1)
    return jnp.where((lane >= head * HDIM) & (lane < (head + 1) * HDIM), 1.0, 0.0)


def by_head(block):
    return jnp.concatenate(
        [block * head_mask(head).astype(jnp.bfloat16) for head in range(HEADS)], axis=0
    )


def together(stacked):
    parts = [stacked[h * SLOT : (h + 1) * SLOT] * head_mask(h) for h in range(HEADS)]
    return functools.reduce(jnp.add, parts).astype(jnp.bfloat16)


def window_bias(last):
    row = lax.broadcasted_iota(jnp.int32, (SLOT, SLOT), 0)
    col = lax.broadcasted_iota(jnp.int32, (SLOT, SLOT), 1)
    bias = jnp.zeros((SLOT, SLOT), jnp.float32)
    if last is not None:
        half = LEV * (WA // 2) * WO
        same = ((row < half) & (col < half)) | ((row >= half) & (col >= half))
        bias = jnp.where(same, 0.0, BLOCKED * last)
    bias = jnp.where(col < SPAN, bias, BLOCKED)
    return jnp.concatenate([bias] * HEADS, axis=0)


def softmax(queries, keys_all, bias):
    scores = dot(queries, keys_all, 1, 1) * HDIM ** (-0.5) + bias
    raised = jnp.exp(scores - jnp.max(scores, axis=-1, keepdims=True))
    return raised / jnp.sum(raised, axis=-1, keepdims=True)


def project_into(target, rows, matrix):
    step = min(512, matrix.shape[0])
    for start in range(0, matrix.shape[0], step):
        part = dot(rows, matrix[start : start + step, :], 1, 1)
        target[:, start : start + step] = part.astype(jnp.bfloat16)


def grad_into(kept, sent, first_row, even, cotan, rows):
    pairs, _, width = kept.shape
    total, columns = cotan.shape[1], rows.shape[1]
    block = total // (2 * pairs)
    step = max(math.lcm(128, 2 * block), 256)
    for start in range(0, total, step):
        part = dot(cotan[:, start : start + step], rows, 0, 0)
        for pair in range(start // (2 * block), (start + step) // (2 * block)):
            at = 2 * pair * block - start
            lower, upper = part[at : at + block], part[at + block : at + 2 * block]
            mine = lax.select(even, lower, upper).astype(jnp.bfloat16)
            other = lax.select(even, upper, lower).astype(jnp.bfloat16)
            for turn in range(columns // width):
                spot = slice(first_row + turn * block, first_row + (turn + 1) * block)
                kept[pair, spot] = mine[:, turn * width : (turn + 1) * width]
                sent[pair, spot] = other[:, turn * width : (turn + 1) * width]


def groups(row_count, channels, lat_windows, last):
    count = row_count // SLOT
    plain = window_bias(None)
    for window in range(count):
        edge = last is not None and window // (count // lat_windows) == lat_windows - 1
        bias = window_bias(last) if edge else plain
        rows = slice(window * SLOT, (window + 1) * SLOT)
        for start in range(0, channels, WIDE):
            yield rows, start, bias


def forward_kernel(lat_windows, shifted, last_ref, x_ref, qkv_ref, out_ref, y_ref, triple, blended):
    last = last_ref[0] if shifted else None
    row_count, channels = x_ref.shape
    project_into(triple, centre(x_ref[...])[0].astype(jnp.bfloat16), qkv_ref)
    for rows, start, bias in groups(row_count, channels, lat_windows, last):
        queries, keys_all, values_all = [
            triple[rows, part * channels + start : part * channels + start + WIDE]
            for part in range(3)
        ]
        weights = softmax(by_head(queries), keys_all, bias).astype(jnp.bfloat16)
        blended[rows, start : start + WIDE] = together(dot(weights, values_all))
    result = dot(blended[...], out_ref[...], 1, 1).astype(jnp.bfloat16)
    y_ref[...] = combine(x_ref[...], result)


def block_back(
    lat_windows, last, even, x, cotan, qkv_ref, out_ref, qkv_pair, out_pair, triple, blended, back
):
    row_count, channels = x.shape
    rows_in = centre(x)[0].astype(jnp.bfloat16)
    project_into(triple, rows_in, qkv_ref)
    cotan_blended = dot(cotan, out_ref[...]).astype(jnp.bfloat16)
    for rows, start, bias in groups(row_count, channels, lat_windows, last):
        spots = [slice(p * channels + start, p * channels + start + WIDE) for p in range(3)]
        queries = by_head(triple[rows, spots[0]])
        keys_all, values_all = triple[rows, spots[1]], triple[rows, spots[2]]
        probs = softmax(queries, keys_all, bias)
        weights = probs.astype(jnp.bfloat16)
        blended[rows, start : start + WIDE] = together(dot(weights, values_all))
        cotan_heads = by_head(cotan_blended[rows, start : start + WIDE])
        cotan_weights = dot(cotan_heads, values_all, 1, 1)
        inner = jnp.sum(probs * cotan_weights, axis=-1, keepdims=True)
        cotan_scores = (probs * (cotan_weights - inner) * HDIM ** (-0.5)).astype(jnp.bfloat16)
        back[rows, spots[0]] = together(dot(cotan_scores, keys_all))
        back[rows, spots[1]] = dot(cotan_scores, queries, 0, 0).astype(jnp.bfloat16)
        back[rows, spots[2]] = dot(weights, cotan_heads, 0, 0).astype(jnp.bfloat16)
    grad_into(*qkv_pair, even, back, rows_in)
    grad_into(*out_pair, even, cotan, blended[...])
    cotan_rows = dot(back[...], qkv_ref[...]).astype(jnp.bfloat16)
    return combine(cotan, norm_back(x, cotan_rows))


def backward_kernel(
    lat_windows, shifted, last_ref, x_ref, cotan_ref, qkv_ref, out_ref,
    cotan_x_ref, kept, sent, triple, blended, back,
):
    last = last_ref[0] if shifted else None
    even = last_ref[1] == 0.0
    qkv_rows = kept.shape[1] * 3 // 4
    cotan_x_ref[...] = block_back(
        lat_windows, last, even, x_ref[...], cotan_ref[...], qkv_ref, out_ref,
        (kept, sent, 0), (kept, sent, qkv_rows), triple, blended, back,
    )


def middle_kernel(
    lat_windows, last_ref, merged_ref, cotan_ref, merge_ref, qkv_ref, out_ref,
    latent_ref, cotan_merged_ref, kept, sent, kept_too, sent_too,
    hidden, triple, blended, back,
):
    even = last_ref[1] == 0.0
    merge_rows = kept_too.shape[1] * 2 // 3
    merged_rows = centre(merged_ref[...])[0].astype(jnp.bfloat16)
    project_into(hidden, merged_rows, merge_ref)
    cotan_hidden = block_back(
        lat_windows, None, even, hidden[...], cotan_ref[...], qkv_ref, out_ref,
        (kept, sent, 0), (kept_too, sent_too, merge_rows), triple, blended, back,
    )
    result = dot(blended[...], out_ref[...], 1, 1).astype(jnp.bfloat16)
    latent_ref[...] = combine(hidden[...], result)
    grad_into(kept_too, sent_too, 0, even, cotan_hidden, merged_rows)
    cotan_rows = dot(cotan_hidden, merge_ref[...]).astype(jnp.bfloat16)
    cotan_merged_ref[...] = norm_back(merged_ref[...], cotan_rows)


def call(kernel, arrays, outs, scratch, flops, name):
    specs = [pl.BlockSpec(memory_space=pltpu.VMEM)] * len(arrays)
    specs[0] = pl.BlockSpec(memory_space=pltpu.SMEM)
    shapes = [jax.ShapeDtypeStruct(shape, jnp.bfloat16) for shape in outs]
    moved = sum(a.size * a.dtype.itemsize for a in arrays) + sum(2 * math.prod(s) for s in outs)
    return pl.pallas_call(
        kernel,
        out_shape=shapes,
        in_specs=specs,
        out_specs=[pl.BlockSpec(memory_space=pltpu.VMEM)] * len(outs),
        scratch_shapes=[pltpu.VMEM(shape, jnp.bfloat16) for shape in scratch],
        compiler_params=pltpu.CompilerParams(vmem_limit_bytes=52 * 2**20),
        cost_estimate=pl.CostEstimate(flops=flops, bytes_accessed=moved, transcendentals=0),
        name=name,
    )(*arrays)


def block_forward(last, rows, w_qkv, w_out, lat_windows, shifted):
    count, channels = rows.shape
    return call(
        functools.partial(forward_kernel, lat_windows, shifted),
        [last, rows, w_qkv, w_out],
        [rows.shape],
        [(count, 3 * channels), rows.shape],
        8 * count * channels * channels,
        "block_forward",
    )[0]


def by_pair(rows, width):
    pairs = lax.axis_size("lat") * lax.axis_size("lon") // 2
    return (pairs, rows // (2 * pairs), width)


def block_backward(last, rows, cotan, w_qkv, w_out, lat_windows, shifted):
    count, channels = rows.shape
    grads = by_pair(4 * channels, channels)
    return call(
        functools.partial(backward_kernel, lat_windows, shifted),
        [last, rows, cotan, w_qkv, w_out],
        [rows.shape, grads, grads],
        [(count, 3 * channels), rows.shape, (count, 3 * channels)],
        24 * count * channels * channels,
        "block_backward",
    )


def middle(last, merged, cotan, w_merge, w_qkv, w_out, lat_windows):
    count, channels = cotan.shape
    grads = by_pair(3 * channels, channels)
    return call(
        functools.partial(middle_kernel, lat_windows),
        [last, merged, cotan, w_merge, w_qkv, w_out],
        [cotan.shape, merged.shape] + [grads] * 4,
        [cotan.shape, (count, 3 * channels), cotan.shape, (count, 3 * channels)],
        36 * count * channels * channels,
        "middle",
    )


def core_sum(kept, sent):
    lon_size = lax.axis_size("lon")
    came = lax.ppermute(sent, "lon", [(i, i ^ 1) for i in range(lon_size)])
    bits = lax.axis_size("lat").bit_length() - 1
    return combine(kept, came).reshape((2,) * bits + (lon_size // 2,) + kept.shape[1:])


def lat_halves(pieces, left, bit):
    dim = left.index(bit)
    mine = lax.div(lax.axis_index("lat"), jnp.int32(2**bit)) % 2
    keep = lax.dynamic_index_in_dim(pieces, mine, dim, keepdims=False)
    return keep, lax.dynamic_index_in_dim(pieces, 1 - mine, dim, keepdims=False)


def lat_order(low_first):
    bits = lax.axis_size("lat").bit_length() - 1
    return list(range(bits)) if low_first else list(reversed(range(bits)))


def all_lat_bits():
    return list(reversed(range(lax.axis_size("lat").bit_length() - 1)))


def start_sum(pair, low_first):
    return lat_halves(core_sum(*pair), all_lat_bits(), lat_order(low_first)[0])


def finish_sum(halves, low_first):
    lat_size, lon_size = lax.axis_size("lat"), lax.axis_size("lon")
    left, order = all_lat_bits(), lat_order(low_first)
    for place, bit in enumerate(order):
        keep, send = halves
        came = lax.ppermute(send, "lat", [(i, i ^ 2**bit) for i in range(lat_size)])
        pieces = combine(keep, came)
        left.remove(bit)
        if left:
            halves = lat_halves(pieces, left, order[place + 1])
    chips = lon_size // 2
    chip = lax.axis_index("lon") // 2
    total = lax.dynamic_index_in_dim(pieces, chip, 0, keepdims=False).astype(jnp.float32)
    for step in range(1, chips):
        send = lax.dynamic_index_in_dim(pieces, (chip + step) % chips, 0, keepdims=False)
        route = [(i, (i + 2 * step) % lon_size) for i in range(lon_size)]
        total = total + lax.ppermute(send, "lon", route).astype(jnp.float32)
    return total


def on_device(
    tokens,
    qkv_first,
    out_first,
    qkv_second,
    out_second,
    merge_weight,
    qkv_third,
    out_third,
    cotangent,
):
    lat_rows, lon_cols = tokens.shape[1:3]
    tall = lat_rows // WA
    edge = lax.axis_index("lat") == lax.axis_size("lat") - 1
    last = jnp.stack([edge, lax.axis_index("lon") % 2 == 1]).astype(jnp.float32)

    rows_one = windows(tokens[0])
    layer_one = block_forward(last, rows_one, qkv_first, out_first, tall, False)
    rows_two = windows(roll_ahead(unwindows(layer_one, lat_rows, lon_cols)))
    layer_two = block_forward(last, rows_two, qkv_second, out_second, tall, True)
    layer_two = roll_behind(unwindows(layer_two, lat_rows, lon_cols))
    merged = windows(merge_patches(layer_two))
    latent, merged_cotan, *third_pairs = middle(
        last, merged, windows(cotangent[0]), merge_weight, qkv_third, out_third, tall // 2
    )
    latent = unwindows(latent, lat_rows // 2, lon_cols // 2)[None]
    third_halves = start_sum(third_pairs[:2], True)
    merge_halves = start_sum(third_pairs[2:], False)

    two_cotan = split_patches(unwindows(merged_cotan, lat_rows // 2, lon_cols // 2))
    two_cotan, *second_pair = block_backward(
        last, rows_two, windows(roll_ahead(two_cotan)), qkv_second, out_second, tall, True
    )
    one_cotan = windows(roll_behind(unwindows(two_cotan, lat_rows, lon_cols)))
    one_cotan, third_halves, merge_halves = lax.optimization_barrier(
        (one_cotan, third_halves, merge_halves)
    )
    one_cotan, *first_pair = block_backward(
        last, rows_one, one_cotan, qkv_first, out_first, tall, False
    )
    tokens_grad = unwindows(one_cotan, lat_rows, lon_cols)[None]
    third_share = finish_sum(third_halves, True)
    merge_share, beside, third_out_share = jnp.split(finish_sum(merge_halves, False), 3, axis=0)
    merge_share = jnp.concatenate([merge_share, beside], axis=1)
    shares = []
    for pair, low_first in ((first_pair, False), (second_pair, True)):
        total = finish_sum(start_sum(pair, low_first), low_first)
        cut = total.shape[0] * 3 // 4
        shares += [total[:cut], total[cut:]]
    shares += [merge_share, third_share, third_out_share]
    return (latent, tokens_grad, *shares)


def solution(mesh):
    placed = (
        P(None, "lat", "lon", None),
        P(),
        P(),
        P(),
        P(),
        P(),
        P(),
        P(),
        P(None, "lat", "lon", None),
    )
    return jax.shard_map(
        on_device,
        mesh=mesh,
        in_specs=placed,
        out_specs=(
            P(None, "lat", "lon", None),
            P(None, "lat", "lon", None),
            P(("lat", "lon"), None),
            P(("lat", "lon"), None),
            P(("lat", "lon"), None),
            P(("lat", "lon"), None),
            P(("lat", "lon"), None),
            P(("lat", "lon"), None),
            P(("lat", "lon"), None),
        ),
        check_vma=False,
    )
```

```python
import functools
import math

import jax
import jax.numpy as jnp
from jax import lax
from jax.experimental import pallas as pl
from jax.experimental.pallas import tpu as pltpu
from jax.sharding import PartitionSpec as P

HDIM = 64
LEV = 1
WA = 6
WO = 12
SPAN = LEV * WA * WO
SLOT = 80
HEADS = 4
WIDE = HEADS * HDIM
BLOCKED = -1e30

EPSILON = 1e-05


def combine(first_term, second_term):
    return (first_term.astype(jnp.float32) + second_term.astype(jnp.float32)).astype(jnp.bfloat16)


def windows(field):
    lat_rows, lon_cols, channels = field.shape
    blocked = field.reshape(lat_rows // WA, WA, lon_cols // WO, WO, channels)
    blocked = blocked.transpose(0, 2, 1, 3, 4).reshape(-1, SPAN, channels)
    return jnp.pad(blocked, ((0, 0), (0, SLOT - SPAN), (0, 0))).reshape(-1, channels)


def unwindows(blocks, lat_rows, lon_cols):
    channels = blocks.shape[-1]
    blocked = blocks.reshape(-1, SLOT, channels)[:, :SPAN]
    blocked = blocked.reshape(lat_rows // WA, lon_cols // WO, WA, WO, channels)
    return blocked.transpose(0, 2, 1, 3, 4).reshape(lat_rows, lon_cols, channels)


def merge_patches(field):
    lat_rows, lon_cols, channels = field.shape
    blocked = field.reshape(lat_rows // 2, 2, lon_cols // 2, 2, channels).transpose(0, 2, 3, 1, 4)
    return blocked.reshape(lat_rows // 2, lon_cols // 2, 4 * channels)


def split_patches(field):
    lat_half, lon_half, four_channels = field.shape
    blocked = field.reshape(lat_half, lon_half, 2, 2, four_channels // 4).transpose(0, 3, 1, 2, 4)
    return blocked.reshape(2 * lat_half, 2 * lon_half, four_channels // 4)


def from_behind(block, axis, distance):
    size = lax.axis_size(axis)
    return lax.ppermute(block, axis, [((i - distance) % size, i) for i in range(size)])


def from_corner(block, distance):
    lats, lons = lax.axis_size("lat"), lax.axis_size("lon")
    route = [
        ((i - distance) % lats * lons + (j - distance) % lons, i * lons + j)
        for i in range(lats)
        for j in range(lons)
    ]
    return lax.ppermute(block, ("lat", "lon"), route)


def roll_ahead(field):
    low, west = WA // 2, WO // 2
    corner = from_corner(field[:low, :west], -1)
    below = from_behind(field[:low, west:], "lat", -1)
    beside = from_behind(field[low:, :west], "lon", -1)
    upper = jnp.concatenate([field[low:, west:], beside], axis=1)
    return jnp.concatenate([upper, jnp.concatenate([below, corner], axis=1)], axis=0)


def roll_behind(field):
    low, west = WA // 2, WO // 2
    corner = from_corner(field[-low:, -west:], 1)
    above = from_behind(field[-low:, :-west], "lat", 1)
    beside = from_behind(field[:-low, -west:], "lon", 1)
    lower = jnp.concatenate([beside, field[:-low, :-west]], axis=1)
    return jnp.concatenate([jnp.concatenate([corner, above], axis=1), lower], axis=0)


def dot(left, right, left_dim=1, right_dim=0):
    return lax.dot_general(
        left, right, (((left_dim,), (right_dim,)), ((), ())), preferred_element_type=jnp.float32
    )


def centre(field):
    values = field.astype(jnp.float32)
    centered = values - jnp.mean(values, axis=-1, keepdims=True)
    inverse = lax.rsqrt(jnp.mean(centered * centered, axis=-1, keepdims=True) + EPSILON)
    return centered * inverse, inverse


def norm_back(field, cotan):
    scaled, inverse = centre(field)
    cotan = cotan.astype(jnp.float32)
    along = jnp.mean(cotan * scaled, axis=-1, keepdims=True)
    return (inverse * (cotan - jnp.mean(cotan, axis=-1, keepdims=True) - scaled * along)).astype(
        jnp.bfloat16
    )


def head_mask(head):
    lane = lax.broadcasted_iota(jnp.int32, (1, WIDE), 1)
    return jnp.where((lane >= head * HDIM) & (lane < (head + 1) * HDIM), 1.0, 0.0)


def by_head(block):
    return jnp.concatenate(
        [block * head_mask(head).astype(jnp.bfloat16) for head in range(HEADS)], axis=0
    )


def together(stacked):
    parts = [stacked[h * SLOT : (h + 1) * SLOT] * head_mask(h) for h in range(HEADS)]
    return functools.reduce(jnp.add, parts).astype(jnp.bfloat16)


def window_bias(last):
    row = lax.broadcasted_iota(jnp.int32, (SLOT, SLOT), 0)
    col = lax.broadcasted_iota(jnp.int32, (SLOT, SLOT), 1)
    bias = jnp.zeros((SLOT, SLOT), jnp.float32)
    if last is not None:
        half = LEV * (WA // 2) * WO
        same = ((row < half) & (col < half)) | ((row >= half) & (col >= half))
        bias = jnp.where(same, 0.0, BLOCKED * last)
    bias = jnp.where(col < SPAN, bias, BLOCKED)
    return jnp.concatenate([bias] * HEADS, axis=0)


def softmax(queries, keys_all, bias):
    scores = dot(queries, keys_all, 1, 1) * HDIM ** (-0.5) + bias
    raised = jnp.exp(scores - jnp.max(scores, axis=-1, keepdims=True))
    return raised / jnp.sum(raised, axis=-1, keepdims=True)


def project_into(target, rows, matrix):
    step = min(512, matrix.shape[0])
    for start in range(0, matrix.shape[0], step):
        part = dot(rows, matrix[start : start + step, :], 1, 1)
        target[:, start : start + step] = part.astype(jnp.bfloat16)


def grad_into(kept, sent, first_row, even, cotan, rows):
    pairs, _, width = kept.shape
    total, columns = cotan.shape[1], rows.shape[1]
    block = total // (2 * pairs)
    step = max(math.lcm(128, 2 * block), 256)
    for start in range(0, total, step):
        part = dot(cotan[:, start : start + step], rows, 0, 0)
        for pair in range(start // (2 * block), (start + step) // (2 * block)):
            at = 2 * pair * block - start
            lower, upper = part[at : at + block], part[at + block : at + 2 * block]
            mine = lax.select(even, lower, upper).astype(jnp.bfloat16)
            other = lax.select(even, upper, lower).astype(jnp.bfloat16)
            for turn in range(columns // width):
                spot = slice(first_row + turn * block, first_row + (turn + 1) * block)
                kept[pair, spot] = mine[:, turn * width : (turn + 1) * width]
                sent[pair, spot] = other[:, turn * width : (turn + 1) * width]


def groups(row_count, channels, lat_windows, last):
    count = row_count // SLOT
    plain = window_bias(None)
    for window in range(count):
        edge = last is not None and window // (count // lat_windows) == lat_windows - 1
        bias = window_bias(last) if edge else plain
        rows = slice(window * SLOT, (window + 1) * SLOT)
        for start in range(0, channels, WIDE):
            yield rows, start, bias


def forward_kernel(lat_windows, shifted, last_ref, x_ref, qkv_ref, out_ref, y_ref, triple, blended):
    last = last_ref[0] if shifted else None
    row_count, channels = x_ref.shape
    project_into(triple, centre(x_ref[...])[0].astype(jnp.bfloat16), qkv_ref)
    for rows, start, bias in groups(row_count, channels, lat_windows, last):
        queries, keys_all, values_all = [
            triple[rows, part * channels + start : part * channels + start + WIDE]
            for part in range(3)
        ]
        weights = softmax(by_head(queries), keys_all, bias).astype(jnp.bfloat16)
        blended[rows, start : start + WIDE] = together(dot(weights, values_all))
    result = dot(blended[...], out_ref[...], 1, 1).astype(jnp.bfloat16)
    y_ref[...] = combine(x_ref[...], result)


def block_back(
    lat_windows, last, even, x, cotan, qkv_ref, out_ref, qkv_pair, out_pair, triple, blended, back
):
    row_count, channels = x.shape
    rows_in = centre(x)[0].astype(jnp.bfloat16)
    project_into(triple, rows_in, qkv_ref)
    cotan_blended = dot(cotan, out_ref[...]).astype(jnp.bfloat16)
    for rows, start, bias in groups(row_count, channels, lat_windows, last):
        spots = [slice(p * channels + start, p * channels + start + WIDE) for p in range(3)]
        queries = by_head(triple[rows, spots[0]])
        keys_all, values_all = triple[rows, spots[1]], triple[rows, spots[2]]
        probs = softmax(queries, keys_all, bias)
        weights = probs.astype(jnp.bfloat16)
        blended[rows, start : start + WIDE] = together(dot(weights, values_all))
        cotan_heads = by_head(cotan_blended[rows, start : start + WIDE])
        cotan_weights = dot(cotan_heads, values_all, 1, 1)
        inner = jnp.sum(probs * cotan_weights, axis=-1, keepdims=True)
        cotan_scores = (probs * (cotan_weights - inner) * HDIM ** (-0.5)).astype(jnp.bfloat16)
        back[rows, spots[0]] = together(dot(cotan_scores, keys_all))
        back[rows, spots[1]] = dot(cotan_scores, queries, 0, 0).astype(jnp.bfloat16)
        back[rows, spots[2]] = dot(weights, cotan_heads, 0, 0).astype(jnp.bfloat16)
    grad_into(*qkv_pair, even, back, rows_in)
    grad_into(*out_pair, even, cotan, blended[...])
    cotan_rows = dot(back[...], qkv_ref[...]).astype(jnp.bfloat16)
    return combine(cotan, norm_back(x, cotan_rows))


def backward_kernel(
    lat_windows, shifted, last_ref, x_ref, cotan_ref, qkv_ref, out_ref,
    cotan_x_ref, kept, sent, triple, blended, back,
):
    last = last_ref[0] if shifted else None
    even = last_ref[1] == 0.0
    qkv_rows = kept.shape[1] * 3 // 4
    cotan_x_ref[...] = block_back(
        lat_windows, last, even, x_ref[...], cotan_ref[...], qkv_ref, out_ref,
        (kept, sent, 0), (kept, sent, qkv_rows), triple, blended, back,
    )


def middle_kernel(
    lat_windows, last_ref, merged_ref, cotan_ref, merge_ref, qkv_ref, out_ref,
    latent_ref, cotan_merged_ref, kept, sent, kept_too, sent_too,
    hidden, triple, blended, back,
):
    even = last_ref[1] == 0.0
    merge_rows = kept_too.shape[1] * 2 // 3
    merged_rows = centre(merged_ref[...])[0].astype(jnp.bfloat16)
    project_into(hidden, merged_rows, merge_ref)
    cotan_hidden = block_back(
        lat_windows, None, even, hidden[...], cotan_ref[...], qkv_ref, out_ref,
        (kept, sent, 0), (kept_too, sent_too, merge_rows), triple, blended, back,
    )
    result = dot(blended[...], out_ref[...], 1, 1).astype(jnp.bfloat16)
    latent_ref[...] = combine(hidden[...], result)
    grad_into(kept_too, sent_too, 0, even, cotan_hidden, merged_rows)
    cotan_rows = dot(cotan_hidden, merge_ref[...]).astype(jnp.bfloat16)
    cotan_merged_ref[...] = norm_back(merged_ref[...], cotan_rows)


def call(kernel, arrays, outs, scratch, flops, name):
    specs = [pl.BlockSpec(memory_space=pltpu.VMEM)] * len(arrays)
    specs[0] = pl.BlockSpec(memory_space=pltpu.SMEM)
    shapes = [jax.ShapeDtypeStruct(shape, jnp.bfloat16) for shape in outs]
    moved = sum(a.size * a.dtype.itemsize for a in arrays) + sum(2 * math.prod(s) for s in outs)
    return pl.pallas_call(
        kernel,
        out_shape=shapes,
        in_specs=specs,
        out_specs=[pl.BlockSpec(memory_space=pltpu.VMEM)] * len(outs),
        scratch_shapes=[pltpu.VMEM(shape, jnp.bfloat16) for shape in scratch],
        compiler_params=pltpu.CompilerParams(vmem_limit_bytes=52 * 2**20),
        cost_estimate=pl.CostEstimate(flops=flops, bytes_accessed=moved, transcendentals=0),
        name=name,
    )(*arrays)


def block_forward(last, rows, w_qkv, w_out, lat_windows, shifted):
    count, channels = rows.shape
    return call(
        functools.partial(forward_kernel, lat_windows, shifted),
        [last, rows, w_qkv, w_out],
        [rows.shape],
        [(count, 3 * channels), rows.shape],
        8 * count * channels * channels,
        "block_forward",
    )[0]


def by_pair(rows, width):
    pairs = lax.axis_size("lat") * lax.axis_size("lon") // 2
    return (pairs, rows // (2 * pairs), width)


def block_backward(last, rows, cotan, w_qkv, w_out, lat_windows, shifted):
    count, channels = rows.shape
    grads = by_pair(4 * channels, channels)
    return call(
        functools.partial(backward_kernel, lat_windows, shifted),
        [last, rows, cotan, w_qkv, w_out],
        [rows.shape, grads, grads],
        [(count, 3 * channels), rows.shape, (count, 3 * channels)],
        24 * count * channels * channels,
        "block_backward",
    )


def middle(last, merged, cotan, w_merge, w_qkv, w_out, lat_windows):
    count, channels = cotan.shape
    grads = by_pair(3 * channels, channels)
    return call(
        functools.partial(middle_kernel, lat_windows),
        [last, merged, cotan, w_merge, w_qkv, w_out],
        [cotan.shape, merged.shape] + [grads] * 4,
        [cotan.shape, (count, 3 * channels), cotan.shape, (count, 3 * channels)],
        36 * count * channels * channels,
        "middle",
    )


def core_sum(kept, sent):
    lon_size = lax.axis_size("lon")
    came = lax.ppermute(sent, "lon", [(i, i ^ 1) for i in range(lon_size)])
    bits = lax.axis_size("lat").bit_length() - 1
    return combine(kept, came).reshape((2,) * bits + (lon_size // 2,) + kept.shape[1:])


def lat_halves(pieces, left, bit):
    dim = left.index(bit)
    mine = lax.div(lax.axis_index("lat"), jnp.int32(2**bit)) % 2
    keep = lax.dynamic_index_in_dim(pieces, mine, dim, keepdims=False)
    return keep, lax.dynamic_index_in_dim(pieces, 1 - mine, dim, keepdims=False)


def lat_order(low_first):
    bits = lax.axis_size("lat").bit_length() - 1
    return list(range(bits)) if low_first else list(reversed(range(bits)))


def all_lat_bits():
    return list(reversed(range(lax.axis_size("lat").bit_length() - 1)))


def start_sum(pair, low_first):
    return lat_halves(core_sum(*pair), all_lat_bits(), lat_order(low_first)[0])


def lat_sum(halves, low_first):
    lat_size = lax.axis_size("lat")
    left, order = all_lat_bits(), lat_order(low_first)
    for place, bit in enumerate(order):
        keep, send = halves
        came = lax.ppermute(send, "lat", [(i, i ^ 2**bit) for i in range(lat_size)])
        pieces = combine(keep, came)
        left.remove(bit)
        if left:
            halves = lat_halves(pieces, left, order[place + 1])
    return pieces


def chip_sum(pieces):
    lon_size = lax.axis_size("lon")
    chips = lon_size // 2
    chip = lax.axis_index("lon") // 2
    total = lax.dynamic_index_in_dim(pieces, chip, 0, keepdims=False).astype(jnp.float32)
    for step in range(1, chips):
        send = lax.dynamic_index_in_dim(pieces, (chip + step) % chips, 0, keepdims=False)
        route = [(i, (i + 2 * step) % lon_size) for i in range(lon_size)]
        total = total + lax.ppermute(send, "lon", route).astype(jnp.float32)
    return total


def split_rows(total, parts):
    unit = total.shape[0] // sum(parts)
    ends = [unit * sum(parts[: place + 1]) for place in range(len(parts))]
    return [total[end - unit * part : end] for end, part in zip(ends, parts)]


def on_device(
    tokens,
    qkv_first,
    out_first,
    qkv_second,
    out_second,
    merge_weight,
    qkv_third,
    out_third,
    cotangent,
):
    lat_rows, lon_cols = tokens.shape[1:3]
    tall = lat_rows // WA
    edge = lax.axis_index("lat") == lax.axis_size("lat") - 1
    last = jnp.stack([edge, lax.axis_index("lon") % 2 == 1]).astype(jnp.float32)

    rows_one = windows(tokens[0])
    layer_one = block_forward(last, rows_one, qkv_first, out_first, tall, False)
    rows_two = windows(roll_ahead(unwindows(layer_one, lat_rows, lon_cols)))
    layer_two = block_forward(last, rows_two, qkv_second, out_second, tall, True)
    layer_two = roll_behind(unwindows(layer_two, lat_rows, lon_cols))
    merged = windows(merge_patches(layer_two))
    latent, merged_cotan, *third_pairs = middle(
        last, merged, windows(cotangent[0]), merge_weight, qkv_third, out_third, tall // 2
    )
    latent = unwindows(latent, lat_rows // 2, lon_cols // 2)[None]
    third_halves = start_sum(third_pairs[:2], True)
    merge_halves = start_sum(third_pairs[2:], False)

    two_cotan = split_patches(unwindows(merged_cotan, lat_rows // 2, lon_cols // 2))
    two_cotan, *second_pair = block_backward(
        last, rows_two, windows(roll_ahead(two_cotan)), qkv_second, out_second, tall, True
    )
    one_cotan = windows(roll_behind(unwindows(two_cotan, lat_rows, lon_cols)))
    one_cotan, third_halves, merge_halves = lax.optimization_barrier(
        (one_cotan, third_halves, merge_halves)
    )
    one_cotan, *first_pair = block_backward(
        last, rows_one, one_cotan, qkv_first, out_first, tall, False
    )
    tokens_grad = unwindows(one_cotan, lat_rows, lon_cols)[None]
    large = [lat_sum(third_halves, True), lat_sum(merge_halves, False)]
    large = jnp.concatenate(large, axis=1)
    starts = zip(start_sum(first_pair, True), start_sum(second_pair, True))
    small = [jnp.concatenate(both, axis=-2) for both in starts]
    large, small = lax.optimization_barrier((large, small))
    third_share, merge_share, beside, third_out_share = split_rows(chip_sum(large), (3, 1, 1, 1))
    merge_share = jnp.concatenate([merge_share, beside], axis=1)
    shares = split_rows(chip_sum(lat_sum(small, True)), (3, 1, 3, 1))
    shares += [merge_share, third_share, third_out_share]
    return (latent, tokens_grad, *shares)


def solution(mesh):
    placed = (
        P(None, "lat", "lon", None),
        P(),
        P(),
        P(),
        P(),
        P(),
        P(),
        P(),
        P(None, "lat", "lon", None),
    )
    return jax.shard_map(
        on_device,
        mesh=mesh,
        in_specs=placed,
        out_specs=(
            P(None, "lat", "lon", None),
            P(None, "lat", "lon", None),
            P(("lat", "lon"), None),
            P(("lat", "lon"), None),
            P(("lat", "lon"), None),
            P(("lat", "lon"), None),
            P(("lat", "lon"), None),
            P(("lat", "lon"), None),
            P(("lat", "lon"), None),
        ),
        check_vma=False,
    )
```
